256 devices in a mesh: section: 4 (over z_lo, core), tile: 64 (over y, x, z_hi).
Axes of the slice: x: 4, y: 4, z: 8 (z_hi: 4, z_lo: 2; z = z_hi * 2 + z_lo), core: 2. Of those that a mesh axis runs over, the one named last changes fastest.
Arguments:
- frames: bfloat16 [3, 64, 8, 10240], P(None, 'tile'), may hold values from -6 to 6
- weights: bfloat16 [4, 3, 3, 256, 512], P('section'), may hold values from -0.75 to 0.75
- bias: bfloat16 [4, 512], P('section'), may hold values from -4 to 4
Outputs:
- hidden_seq: bfloat16 [4, 3, 64, 8, 10240], P('section', None, 'tile')
- final_cell: float32 [4, 64, 8, 10240], P('section', 'tile')
The draws below stay inside these ranges and needn't reach their ends.
All inputs are finite; a program needn't handle non-finite values.
Results may differ from the reference program's by a relative error of at most 0.008.
Values may be sent and summed in bfloat16 or wider, within the bound.
A program may use at most 64 MiB of HBM per device.

```python
import jax
import jax.numpy as jnp

C = 128
CX = 80
CY = 8
TIME = 3
TCOLS = 8
TILES = 64
LAYERS = 4
NY = 64
NX = 640
N_SECTION = 4
N_TILE = 64


def levels(own_key, extent, pieces, low, largest):
    def one(position, shards_of):
        draws = jax.random.uniform(jax.random.fold_in(jax.random.fold_in(own_key, 6), position), (shards_of,), jnp.float32, low / len(pieces), largest / len(pieces))
        return jnp.repeat(jnp.exp(draws), extent[position] // shards_of).reshape((-1,) + (1,) * (len(extent) - position - 1))

    gain = one(*pieces[0])
    for cut in pieces[1:]:
        gain = gain * one(*cut)
    return gain


def noise(key, extent, deviation, limit, cuts=(), kind=jnp.bfloat16):
    loudness = levels(key, extent, cuts, -0.22, 0.18) if cuts else 1.0
    values = jax.random.normal(key, extent, jnp.float32) * deviation * loudness
    return jnp.minimum(jnp.maximum(values, -limit), limit).astype(kind)


def setup_inputs(seed: int = 0) -> dict:
    arg_keys = jax.random.split(jax.random.key(seed), 4)
    frames = noise(arg_keys[0], (TIME, TILES, CY, CX * C), 1.0, 6.0, ((1, 64),))
    weights = noise(arg_keys[1], (LAYERS, 3, 3, 2 * C, 4 * C), (C // 2) ** -0.5, 0.75, ((0, 4),))
    bias = noise(arg_keys[2], (LAYERS, 4 * C), 0.3, 4.0, ((0, 4),))
    return {"frames": frames, "weights": weights, "bias": bias}


def to_grid(array):
    lead = array.shape[:-3]
    count = len(lead)
    rows = N_TILE // TCOLS
    array = array.reshape(lead + (rows, TCOLS, CY, CX, C))
    order = list(range(count)) + [count, count + 2, count + 1, count + 3, count + 4]
    return array.transpose(order).reshape(lead + (rows * CY, TCOLS * CX, C))


def from_grid(array):
    lead = array.shape[:-3]
    count = len(lead)
    rows = N_TILE // TCOLS
    array = array.reshape(lead + (rows, CY, TCOLS, CX, C))
    order = list(range(count)) + [count, count + 2, count + 1, count + 3, count + 4]
    return array.transpose(order).reshape(lead + (rows * TCOLS, CY, CX * C))


def reference(frames, weights, bias):
    grid = to_grid(frames)
    inputs = [grid[step] for step in range(TIME)]
    hidden_all = []
    cell_all = []
    for layer in range(N_SECTION):
        hidden = jnp.zeros((NY, NX, C), jnp.bfloat16)
        cell = jnp.zeros((NY * NX, C), jnp.float32)
        outputs = []
        for step in range(TIME):
            joined = jnp.concatenate([inputs[step], hidden], axis=-1)
            padded = jnp.pad(joined, ((1, 1), (1, 1), (0, 0)))
            gates = jnp.zeros((NY * NX, 4 * C), jnp.float32) + bias[layer].astype(jnp.float32)
            for row_off in range(3):
                for col_off in range(3):
                    window = padded[row_off:row_off + NY, col_off:col_off + NX].reshape(NY * NX, 2 * C)
                    gates = gates + jnp.dot(window, weights[layer, row_off, col_off], preferred_element_type=jnp.float32)
            cell = jax.nn.sigmoid(gates[:, C:2 * C]) * cell + jax.nn.sigmoid(gates[:, :C]) * jnp.tanh(gates[:, 3 * C:])
            hidden = (jax.nn.sigmoid(gates[:, 2 * C:3 * C]) * jnp.tanh(cell)).astype(jnp.bfloat16).reshape(NY, NX, C)
            outputs.append(hidden)
        inputs = outputs
        hidden_all.append(jnp.stack(outputs))
        cell_all.append(cell.reshape(NY, NX, C))
    return from_grid(jnp.stack(hidden_all)), from_grid(jnp.stack(cell_all))
```

```python
import functools

import jax
import jax.numpy as jnp
from jax import lax
from jax.experimental import pallas as pl
from jax.experimental.pallas import tpu as pltpu
from jax.sharding import PartitionSpec as P

MESH = pl.DeviceIdType.MESH
TCOLS = 8
TROWS = 8
C = 128
CX, CY, TIME = 80, 8, 3
HALF = CX // 2
TOP = 4
ROWS = CY + 2 * TOP
WIDE = 48
FIRST = 64
FW = 80
IW = 88
CHUNKS = {14: (4, 3, 3, 4), 12: (4, 4, 4), 10: (5, 5), 8: (4, 4)}
BF, F32 = jnp.bfloat16, jnp.float32


def sigmoid(v):
    return 0.5 * jnp.tanh(0.5 * v) + 0.5


def kernel(
    frames, weights, bias, out_h, out_c,
    fr, s32, fyb, hb, hz, fin, zin0, zin, zh, f0, f1, cell, wv, bv, hs, cs,
    local_sem, w_send, w_recv, fr_send, fr_recv, z_send, z_recv, o_send, o_recv,
):
    section, tile = lax.axis_index("section"), lax.axis_index("tile")
    stage, core = section // 2, section % 2
    first_stage = stage == 0
    row, col = tile // TCOLS, tile % TCOLS
    has_n, has_s = row > 0, row < TROWS - 1
    has_side = jnp.where(core == 0, col > 0, col < TCOLS - 1)
    side = 2 * core - 1
    partner = (2 * stage + 1 - core, tile)

    def at(stage_of, core_of, tile_of):
        return (2 * stage_of + core_of, tile_of)

    own_w = [
        pltpu.make_async_copy(
            weights.at[0, :, :, pl.ds(C * p, C), :], wv.at[core, :, :, pl.ds(C * p, C), :], local_sem.at[p]
        )
        for p in range(2)
    ]
    load_f = pltpu.make_async_copy(frames.at[:, 0], fr, local_sem.at[2])

    @pl.when(first_stage)
    def _():
        load_f.start()

    for cp in own_w:
        cp.start()

    def bias_copy():
        return pltpu.make_async_remote_copy(
            src_ref=bv.at[core], dst_ref=bv.at[core], send_sem=w_send.at[2], recv_sem=w_recv.at[2],
            device_id=partner, device_id_type=MESH,
        )

    def weight_copy(p):
        return pltpu.make_async_remote_copy(
            src_ref=weights.at[0, :, :, pl.ds(C * p, C), :], dst_ref=wv.at[core, :, :, pl.ds(C * p, C), :],
            send_sem=w_send.at[p], recv_sem=w_recv.at[p], device_id=partner, device_id_type=MESH,
        )

    cols48 = pl.multiple_of(32 * core, 16)
    to48 = pl.multiple_of(16 * (1 - core), 16)
    cols16 = pl.multiple_of(64 * core, 16)
    to16 = pl.multiple_of(48 * (1 - core), 16)

    def frame_copies(t):
        n = TOP - t

        def copy(kind, from_row, to_row, count, wide, target):
            src = fyb.at[t, pl.ds(from_row, count), pl.ds(cols48, WIDE) if wide else pl.ds(cols16, 16)]
            dst = hb.at[t, pl.ds(to_row, count), pl.ds(to48, WIDE) if wide else pl.ds(to16, 16)]
            return pltpu.make_async_remote_copy(
                src_ref=src, dst_ref=dst, send_sem=fr_send.at[t, kind], recv_sem=fr_recv.at[t, kind],
                device_id=target, device_id_type=MESH,
            )

        return [
            (has_s, has_n, copy(0, CY - n, TOP - n, n, True, at(0, core, tile + TCOLS))),
            (has_n, has_s, copy(1, 0, TOP + CY, n, True, at(0, core, tile - TCOLS))),
            (has_side, has_side, copy(2, 0, TOP, CY, False, at(0, 1 - core, tile + side))),
            (has_side & has_s, has_side & has_n, copy(3, CY - n, TOP - n, n, False, at(0, 1 - core, tile + side + TCOLS))),
            (has_side & has_n, has_side & has_s, copy(4, 0, TOP + CY, n, False, at(0, 1 - core, tile + side - TCOLS))),
        ]

    def own_frame(t):
        return pltpu.make_async_copy(
            fyb.at[t, :, pl.ds(cols48, WIDE)], hb.at[t, pl.ds(TOP, CY), pl.ds(to48, WIDE)], local_sem.at[4 + t]
        )

    def stage_copies(t):
        k = TIME - 1 - t

        def copy(kind, from_row, to_row, count, target):
            return pltpu.make_async_remote_copy(
                src_ref=zh.at[1, t, 1, pl.ds((TOP + from_row) * WIDE, count * WIDE)],
                dst_ref=hz.at[t, pl.ds((TOP + to_row) * WIDE, count * WIDE)],
                send_sem=z_send.at[t, kind], recv_sem=z_recv.at[t, kind], device_id=target, device_id_type=MESH,
            )

        return [
            (has_s, has_n, copy(0, CY - 2 - k, -2 - k, 2, at(1, core, tile + TCOLS))),
            (has_n, has_s, copy(1, k, CY + k, 2, at(1, core, tile - TCOLS))),
            (None, None, copy(2, -k, -k, CY + 2 * k, at(1, core, tile))),
        ]

    def when(condition, action):
        if condition is None:
            action()
        else:
            pl.when(condition)(action)

    bv[core] = jnp.broadcast_to(bias[...].astype(F32), (8, 4 * C))
    f0[...] = jnp.zeros_like(f0)
    f1[...] = jnp.zeros_like(f1)
    fin[...] = jnp.zeros_like(fin)

    @pl.when(first_stage)
    def _():
        hb[...] = jnp.zeros_like(hb)
        load_f.wait()
        for t in range(TIME):
            for x in range(CX):
                s32[CY * x : CY * (x + 1), :] = fr[t, :, C * x : C * (x + 1)].astype(F32)
            for y in range(CY):
                fyb[t, y] = s32[pl.ds(y, CX, stride=CY), :].astype(BF)
            own_frame(t).start()

    @pl.when(jnp.logical_not(first_stage))
    def _():
        hz[...] = jnp.zeros_like(hz)

    barrier = pltpu.get_barrier_semaphore()

    def greet(device):
        pl.semaphore_signal(barrier, inc=1, device_id=device, device_id_type=MESH)

    def met():
        pl.semaphore_wait(barrier, 1)

    greet(partner)
    greet(at(1 - stage, core, tile))
    pl.when(has_n)(lambda: greet(at(1 - stage, core, tile - TCOLS)))
    pl.when(has_s)(lambda: greet(at(1 - stage, core, tile + TCOLS)))

    @pl.when(first_stage)
    def _():
        pl.when(has_n)(lambda: greet(at(0, core, tile - TCOLS)))
        pl.when(has_s)(lambda: greet(at(0, core, tile + TCOLS)))
        pl.when(has_side)(lambda: greet(at(0, 1 - core, tile + side)))
        pl.when(has_side & has_n)(lambda: greet(at(0, 1 - core, tile + side - TCOLS)))
        pl.when(has_side & has_s)(lambda: greet(at(0, 1 - core, tile + side + TCOLS)))

    one = lambda c: c.astype(jnp.int32)
    near = one(has_n) + one(has_s)
    mine = 2 + near
    tiles = near + one(has_side) + one(has_side & has_n) + one(has_side & has_s)
    pl.semaphore_wait(barrier, mine + jnp.where(first_stage, tiles, 0))

    bias_copy().start()

    @pl.when(first_stage)
    def _():
        for sends, _, cp in frame_copies(0):
            pl.when(sends)(cp.start)

    weight_copy(0).start()

    @pl.when(first_stage)
    def _():
        for t in range(1, TIME):
            for sends, _, cp in frame_copies(t):
                pl.when(sends)(cp.start)

    weight_copy(1).start()

    def column_mask(width, first):
        x = lax.broadcasted_iota(jnp.int32, (width, C), 0) + (first + HALF * core + CX * col)
        return (x >= 0) & (x < CX * TCOLS)

    masks = {WIDE: column_mask(WIDE, -4), FIRST: column_mask(FIRST, -12)}

    def put_input(t, first_column):
        width = FIRST if t == 0 else WIDE
        target = zin0 if t == 0 else zin.at[t - 1]
        for y in range(t, ROWS - t):
            for b in range(3):
                begin = y * IW + first_column + b - 1
                target[b, y * width : (y + 1) * width, :] = fin[begin : begin + width, :].astype(BF)

    def get_input(t):
        @pl.when(first_stage)
        def _():
            own_frame(t).wait()
            for _, gets, cp in frame_copies(t):
                pl.when(gets)(cp.wait_recv)
            for y in range(t, ROWS - t):
                fin[pl.ds(pl.multiple_of(y * IW + 8 + 8 * core, 8), FIRST), :] = hb[t, y].astype(F32)
            put_input(t, 12 if t == 0 else 20)

        @pl.when(jnp.logical_not(first_stage))
        def _():
            for _, gets, cp in stage_copies(t):
                when(gets, cp.wait_recv)
            for y in range(t, ROWS - t):
                fin[y * IW + 24 : y * IW + 24 + WIDE, :] = hz[t, y * WIDE : (y + 1) * WIDE, :].astype(F32)
            put_input(t, 16 if t == 0 else 24)

    def step(layer, t):
        k = (1 - layer) + (TIME - 1 - t)
        width = FIRST if (layer == 0 and t == 0) else WIDE
        hidden = f0 if layer == 0 else f1
        if layer == 1:
            source = zh.at[0, t]
        else:
            source = zin0 if t == 0 else zin.at[t - 1]
        if t == 0:
            kernel_of = wv[layer, :, :, :C, :].reshape(9 * C, 4 * C)
        else:
            kernel_of = wv[layer].reshape(18 * C, 4 * C)
        gate_bias = bv[layer, 0:1, :]
        y = -k
        for count in CHUNKS[CY + 2 * k]:
            pieces = []
            for a in range(3):
                rows = pl.ds((y + a - 1 + TOP) * width, count * width)
                for b in range(3):
                    pieces.append(source[b, rows, :])
                    if t > 0:
                        pieces.append(zh[layer, t - 1, b, rows, :])
            gates = jnp.dot(jnp.concatenate(pieces, axis=1), kernel_of, preferred_element_type=F32) + gate_bias
            c_new = sigmoid(gates[:, :C]) * jnp.tanh(gates[:, 3 * C :])
            cells = pl.ds((y + TOP) * WIDE, count * WIDE)
            if t > 0:
                c_new = sigmoid(gates[:, C : 2 * C]) * cell[layer, cells, :] + c_new
            h_new = sigmoid(gates[:, 2 * C : 3 * C]) * jnp.tanh(c_new)
            for i in range(count):
                line = y + i
                inside = masks[width]
                if line < 0:
                    inside = inside & has_n
                if line >= CY:
                    inside = inside & has_s
                h_row = jnp.where(inside, h_new[i * width : (i + 1) * width, :], 0.0)
                begin = (line + TOP) * FW + 16
                edge = (width - WIDE) // 2
                hidden[begin - edge : begin + WIDE + edge, :] = h_row
                cell[layer, (line + TOP) * WIDE : (line + TOP + 1) * WIDE, :] = c_new[i * width + edge : (i + 1) * width - edge, :]
                for b in range(3):
                    zh[layer, t, b, (line + TOP) * WIDE : (line + TOP + 1) * WIDE, :] = hidden[
                        begin + b - 1 : begin + b - 1 + WIDE, :
                    ].astype(BF)
            y += count

    def result_copies(layer, src, dst, slot):
        local = pltpu.make_async_copy(src, dst, local_sem.at[8 + slot])
        remote = pltpu.make_async_remote_copy(
            src_ref=src, dst_ref=dst, send_sem=o_send.at[slot], recv_sem=o_recv.at[slot],
            device_id=partner, device_id_type=MESH,
        )
        return core == layer, local, remote

    half = pl.ds(pl.multiple_of(core * (HALF * C), C), HALF * C)

    def hidden_copies(layer, t):
        return result_copies(layer, hs.at[layer, t], out_h.at[0, t, 0, :, half], t)

    def cell_copies(layer):
        return result_copies(layer, cs.at[layer], out_c.at[0, 0, :, half], TIME)

    def send(copies):
        here, local, remote = copies
        pl.when(here)(local.start)
        pl.when(jnp.logical_not(here))(remote.start)

    def finish(copies):
        here, local, remote = copies

        @pl.when(here)
        def _():
            local.wait()
            remote.wait_recv()

        pl.when(jnp.logical_not(here))(remote.wait_send)

    def put_hidden(layer, t):
        hidden = f0 if layer == 0 else f1
        for x in range(HALF):
            hs[layer, t, :, C * x : C * (x + 1)] = hidden[pl.ds(TOP * FW + 20 + x, CY, stride=FW), :].astype(BF)
        send(hidden_copies(layer, t))

    def put_cell(layer):
        for x in range(HALF):
            cs[layer, :, C * x : C * (x + 1)] = cell[layer, pl.ds(TOP * WIDE + 4 + x, CY, stride=WIDE), :]
        send(cell_copies(layer))

    for p in range(2):
        own_w[p].wait()
    for t in range(TIME):
        get_input(t)
        if t == 0:
            bias_copy().wait_recv()
            weight_copy(0).wait_recv()
        if t == 1:
            weight_copy(1).wait_recv()
        step(0, t)
        step(1, t)

        @pl.when(first_stage)
        def _(t=t):
            for sends, _, cp in stage_copies(t):
                when(sends, cp.start)

        put_hidden(0, t)
        put_hidden(1, t)
    put_cell(0)
    put_cell(1)

    bias_copy().wait_send()
    for p in range(2):
        weight_copy(p).wait_send()

    @pl.when(first_stage)
    def _():
        for t in range(TIME):
            for sends, _, cp in frame_copies(t) + stage_copies(t):
                when(sends, cp.wait_send)

    for layer in range(2):
        for t in range(TIME):
            finish(hidden_copies(layer, t))
        finish(cell_copies(layer))


def local(frames, weights, bias):
    any_space = pl.BlockSpec(memory_space=pl.ANY)
    dma = pltpu.SemaphoreType.DMA
    return pl.pallas_call(
        kernel,
        out_shape=(
            jax.ShapeDtypeStruct((1, TIME, 1, CY, CX * C), BF),
            jax.ShapeDtypeStruct((1, 1, CY, CX * C), F32),
        ),
        in_specs=[any_space, any_space, pl.BlockSpec(memory_space=pltpu.VMEM)],
        out_specs=(any_space, any_space),
        scratch_shapes=[
            pltpu.VMEM((TIME, CY, CX * C), BF),
            pltpu.VMEM((CY * CX, C), F32),
            pltpu.VMEM((TIME, CY, CX, C), BF),
            pltpu.VMEM((TIME, ROWS, FIRST, C), BF),
            pltpu.VMEM((TIME, ROWS * WIDE, C), BF),
            pltpu.VMEM((ROWS * IW, C), F32),
            pltpu.VMEM((3, ROWS * FIRST, C), BF),
            pltpu.VMEM((TIME - 1, 3, ROWS * WIDE, C), BF),
            pltpu.VMEM((2, TIME, 3, ROWS * WIDE, C), BF),
            pltpu.VMEM((ROWS * FW, C), F32),
            pltpu.VMEM((ROWS * FW, C), F32),
            pltpu.VMEM((2, ROWS * WIDE, C), F32),
            pltpu.VMEM((2, 3, 3, 2 * C, 4 * C), BF),
            pltpu.VMEM((2, 8, 4 * C), F32),
            pltpu.VMEM((2, TIME, CY, HALF * C), BF),
            pltpu.VMEM((2, CY, HALF * C), F32),
            dma((12,)),
            dma((3,)),
            dma((3,)),
            dma((TIME, 5)),
            dma((TIME, 5)),
            dma((TIME, 3)),
            dma((TIME, 3)),
            dma((TIME + 1,)),
            dma((TIME + 1,)),
        ],
        compiler_params=pltpu.CompilerParams(
            collective_id=0, has_side_effects=True, vmem_limit_bytes=48 * 2**20
        ),
    )(frames, weights, bias)


def solution(mesh):
    return jax.shard_map(
        local,
        mesh=mesh,
        in_specs=(P(None, "tile", None, None), P("section", None, None, None, None), P("section", None)),
        out_specs=(P("section", None, "tile", None, None), P("section", "tile", None, None)),
        check_vma=False,
    )
```

```python
import functools

import jax
import jax.numpy as jnp
from jax import lax
from jax.experimental import pallas as pl
from jax.experimental.pallas import tpu as pltpu
from jax.sharding import PartitionSpec as P

MESH = pl.DeviceIdType.MESH
TCOLS = 8
TROWS = 8
C = 128
CX, CY, TIME = 80, 8, 3
HALF = CX // 2
TOP = 4
ROWS = CY + 2 * TOP
WIDE = 48
FIRST = 64
FW = 80
IW = 88
CHUNKS = ({14: (4, 3, 3, 4), 12: (4, 4, 4), 10: (4, 3, 3)}, {12: (6, 6), 10: (5, 5), 8: (4, 4)})
OWN = (((-2, 4), (2, 4), (6, 4)), ((-1, 4), (3, 3), (6, 3)), ((0, 2), (6, 2), (2, 4)))
BF, F32 = jnp.bfloat16, jnp.float32


def sigmoid(v):
    return 0.5 * jnp.tanh(0.5 * v) + 0.5


def kernel(
    frames, weights, bias, out_h, out_c,
    fr, s32, fyb, hb, hz, fin, zin0, zin, zh, hid, cell, part0, part1, wv, bv, hs, cs,
    local_sem, w_send, w_recv, fr_send, fr_recv, z_send, z_recv, o_send, o_recv,
):
    section, tile = lax.axis_index("section"), lax.axis_index("tile")
    stage, core = section // 2, section % 2
    first_stage = stage == 0
    row, col = tile // TCOLS, tile % TCOLS
    has_n, has_s = row > 0, row < TROWS - 1
    has_side = jnp.where(core == 0, col > 0, col < TCOLS - 1)
    side = 2 * core - 1
    partner = (2 * stage + 1 - core, tile)

    def at(stage_of, core_of, tile_of):
        return (2 * stage_of + core_of, tile_of)

    own_w = [
        pltpu.make_async_copy(
            weights.at[0, :, :, pl.ds(C * p, C), :], wv.at[core, :, :, pl.ds(C * p, C), :], local_sem.at[p]
        )
        for p in range(2)
    ]
    load_f = pltpu.make_async_copy(frames.at[:, 0], fr, local_sem.at[2])

    @pl.when(first_stage)
    def _():
        load_f.start()

    for cp in own_w:
        cp.start()

    def bias_copy():
        return pltpu.make_async_remote_copy(
            src_ref=bv.at[core], dst_ref=bv.at[core], send_sem=w_send.at[2], recv_sem=w_recv.at[2],
            device_id=partner, device_id_type=MESH,
        )

    def weight_copy(p):
        return pltpu.make_async_remote_copy(
            src_ref=weights.at[0, :, :, pl.ds(C * p, C), :], dst_ref=wv.at[core, :, :, pl.ds(C * p, C), :],
            send_sem=w_send.at[p], recv_sem=w_recv.at[p], device_id=partner, device_id_type=MESH,
        )

    cols48 = pl.multiple_of(32 * core, 16)
    to48 = pl.multiple_of(16 * (1 - core), 16)
    cols16 = pl.multiple_of(64 * core, 16)
    to16 = pl.multiple_of(48 * (1 - core), 16)

    def frame_copies(t):
        n = TOP - t

        def copy(kind, from_row, to_row, count, wide, target):
            src = fyb.at[t, pl.ds(from_row, count), pl.ds(cols48, WIDE) if wide else pl.ds(cols16, 16)]
            dst = hb.at[t, pl.ds(to_row, count), pl.ds(to48, WIDE) if wide else pl.ds(to16, 16)]
            return pltpu.make_async_remote_copy(
                src_ref=src, dst_ref=dst, send_sem=fr_send.at[t, kind], recv_sem=fr_recv.at[t, kind],
                device_id=target, device_id_type=MESH,
            )

        return [
            (has_side & has_s, has_side & has_n, copy(3, CY - n, TOP - n, n, False, at(0, 1 - core, tile + side + TCOLS))),
            (has_side & has_n, has_side & has_s, copy(4, 0, TOP + CY, n, False, at(0, 1 - core, tile + side - TCOLS))),
            (has_s, has_n, copy(0, CY - n, TOP - n, n, True, at(0, core, tile + TCOLS))),
            (has_n, has_s, copy(1, 0, TOP + CY, n, True, at(0, core, tile - TCOLS))),
            (has_side, has_side, copy(2, 0, TOP, CY, False, at(0, 1 - core, tile + side))),
        ]

    def stage_copies(t, receiving=False):
        k = TIME - 1 - t

        def copy(kind, from_row, to_row, count, target, lands=None):
            lands = kind if receiving or lands is None else lands
            return pltpu.make_async_remote_copy(
                src_ref=zh.at[1, t, 1, pl.ds((TOP + from_row) * WIDE, count * WIDE)],
                dst_ref=hz.at[t, pl.ds(pl.multiple_of((TOP + to_row) * WIDE, WIDE), count * WIDE)],
                send_sem=z_send.at[t, kind], recv_sem=z_recv.at[t, lands], device_id=target, device_id_type=MESH,
            )

        unread = CY + TOP
        return [
            copy(
                0, CY - 2 - k, jnp.where(has_s, -2 - k, unread), 2, at(1, core, jnp.where(has_s, tile + TCOLS, tile)),
                jnp.where(has_s, 0, 1),
            ),
            copy(
                1, k, jnp.where(has_n, CY + k, unread), 2, at(1, core, jnp.where(has_n, tile - TCOLS, tile)),
                jnp.where(has_n, 1, 0),
            ),
            *[copy(2 + i, y, y, count, at(1, core, tile)) for i, (y, count) in enumerate(OWN[t])],
        ]

    def put_input(t, rows, width, first_column, low=0, count=None):
        target = zin0 if width == FIRST else zin.at[t]
        count = width if count is None else count
        for y in rows:
            for b in range(3):
                begin = y * IW + first_column + low + b - 1
                target[b, y * width + low : y * width + low + count, :] = fin[t, begin : begin + count, :].astype(BF)

    def frame_width(t):
        return (FIRST, 12) if t == 0 else (WIDE, 20)

    own_rows = range(TOP, TOP + CY)

    def await_frame(t):
        for _, gets, cp in frame_copies(t):
            pl.when(gets)(cp.wait_recv)

    def get_frame(t):
        halo_rows = [*range(t, TOP), *range(TOP + CY, ROWS - t)]
        width, first_column = frame_width(t)
        for y in halo_rows:
            fin[t, pl.ds(pl.multiple_of(y * IW + 8 + 8 * core, 8), FIRST), :] = hb[t, y].astype(F32)
        for y in own_rows:
            fin[t, pl.ds(pl.multiple_of(y * IW + 8 + 56 * core, 8), 16), :] = hb[
                t, y, pl.ds(pl.multiple_of(48 * core, 16), 16), :
            ].astype(F32)
        put_input(t, halo_rows, width, first_column)
        put_input(t, own_rows, width, first_column, 0, 16)
        put_input(t, own_rows, width, first_column, width - 16, 16)

    def get_hidden(t):
        k = TIME - 1 - t
        copies = stage_copies(t, receiving=True)
        parts = [(copies[2 + i : 3 + i], range(y, y + count)) for i, (y, count) in enumerate(OWN[t])]
        parts.append((copies[:2], [-2 - k, -1 - k, CY + k, CY + k + 1]))
        for waits, lines in parts:
            for cp in waits:
                cp.wait_recv()
            rows = [TOP + line for line in lines]
            for y in rows:
                fin[t, y * IW + 24 : y * IW + 24 + WIDE, :] = hz[t, y * WIDE : (y + 1) * WIDE, :].astype(F32)
            put_input(t, rows, WIDE, 24)

    @pl.when(first_stage)
    def _():
        @pl.when(jnp.logical_not(has_n & has_s & has_side))
        def _():
            hb[...] = jnp.zeros_like(hb)

    @pl.when(jnp.logical_not(first_stage))
    def _():
        hz[...] = jnp.zeros_like(hz)

    barrier = pltpu.get_barrier_semaphore()

    def greet(device):
        pl.semaphore_signal(barrier, inc=1, device_id=device, device_id_type=MESH)

    @pl.when(first_stage)
    def _():
        pl.when(has_side & has_n)(lambda: greet(at(0, 1 - core, tile + side - TCOLS)))
        pl.when(has_side & has_s)(lambda: greet(at(0, 1 - core, tile + side + TCOLS)))
        pl.when(has_side)(lambda: greet(at(0, 1 - core, tile + side)))
        pl.when(has_n)(lambda: greet(at(0, core, tile - TCOLS)))
        pl.when(has_s)(lambda: greet(at(0, core, tile + TCOLS)))

    pl.when(has_n)(lambda: greet(at(1 - stage, core, tile - TCOLS)))
    pl.when(has_s)(lambda: greet(at(1 - stage, core, tile + TCOLS)))
    greet(at(1 - stage, core, tile))
    greet(partner)

    def put_rows(t):
        for x in range(CX):
            s32[CY * x : CY * (x + 1), :] = fr[t, :, C * x : C * (x + 1)].astype(F32)
        for y in range(CY):
            fyb[t, y] = s32[pl.ds(y, CX, stride=CY), :].astype(BF)

    def send_frame(t):
        for sends, _, cp in frame_copies(t):
            pl.when(sends)(cp.start)

    bv[core] = jnp.broadcast_to(bias[...].astype(F32), (8, 4 * C))

    @pl.when(first_stage)
    def _():
        load_f.wait()
        put_rows(0)

    one = lambda c: c.astype(jnp.int32)
    near = one(has_n) + one(has_s)
    mine = 2 + near
    tiles = near + one(has_side) + one(has_side & has_n) + one(has_side & has_s)
    pl.semaphore_wait(barrier, mine + jnp.where(first_stage, tiles, 0))

    @pl.when(first_stage)
    def _():
        send_frame(0)

    bias_copy().start()
    weight_copy(0).start()

    @pl.when(first_stage)
    def _():
        put_rows(1)
        send_frame(1)
        put_rows(2)
        send_frame(2)

    weight_copy(1).start()

    hid[...] = jnp.zeros_like(hid)
    fin[...] = jnp.zeros_like(fin)

    @pl.when(first_stage)
    def _():
        for t in range(TIME):
            for y in range(CY):
                fin[t, pl.ds(pl.multiple_of((y + TOP) * IW + 24 - 8 * core, 8), WIDE), :] = fyb[
                    t, y, pl.ds(cols48, WIDE), :
                ].astype(F32)
            width, first_column = frame_width(t)
            put_input(t, own_rows, width, first_column, 16, width - 32)

    def column_mask(width, first):
        x = lax.broadcasted_iota(jnp.int32, (width, C), 0) + (first + HALF * core + CX * col)
        return (x >= 0) & (x < CX * TCOLS)

    masks = {WIDE: column_mask(WIDE, -4), FIRST: column_mask(FIRST, -12)}

    def taps(groups, width, array):
        pieces = []
        for a in range(3):
            for b in range(3):
                rows = [array[b, pl.ds((y + a - 1 + TOP) * width, count * width), :] for y, count in groups]
                pieces.append(rows[0] if len(rows) == 1 else jnp.concatenate(rows, axis=0))
        return jnp.concatenate(pieces, axis=1)

    def all_rows(layer, t):
        y = -((1 - layer) + (TIME - 1 - t))
        chunks = []
        for count in CHUNKS[layer][CY - 2 * y]:
            chunks.append([(y, count)])
            y += count
        return chunks

    parts = (part0, part1)

    def hidden_part(layer, t):
        k = (1 - layer) + (TIME - 1 - t)
        for groups in all_rows(layer, t):
            ((y, count),) = groups
            parts[layer][(y + k) * WIDE : (y + k + count) * WIDE, :] = jnp.dot(
                taps(groups, WIDE, zh.at[layer, t - 1]),
                wv[layer, :, :, C:, :].reshape(9 * C, 4 * C),
                preferred_element_type=F32,
            )

    def step(layer, t, width=WIDE, split=False, chunks=None):
        k = (1 - layer) + (TIME - 1 - t)
        split = split and t > 0
        whole = t > 0 and not split
        source = zh.at[0, t] if layer == 1 else (zin0 if width == FIRST else zin.at[t])

        def chunk(groups):
            columns = taps(groups, width, source)
            factors = wv[layer, :, :, :C, :].reshape(9 * C, 4 * C)
            if whole:
                columns = jnp.concatenate([taps(groups, width, zh.at[layer, t - 1]), columns], axis=1)
                factors = jnp.concatenate([wv[layer, :, :, C:, :].reshape(9 * C, 4 * C), factors], axis=0)
            gates = jnp.dot(columns, factors, preferred_element_type=F32) + bv[layer, 0:1, :]
            if split:
                gates = gates + parts[layer][(groups[0][0] + k) * WIDE : (groups[0][0] + k + groups[0][1]) * WIDE, :]
            c_new = sigmoid(gates[:, :C]) * jnp.tanh(gates[:, 3 * C :])
            if t > 0:
                old = [cell[layer, pl.ds((y + TOP) * WIDE, count * WIDE), :] for y, count in groups]
                old = old[0] if len(old) == 1 else jnp.concatenate(old, axis=0)
                c_new = sigmoid(gates[:, C : 2 * C]) * old + c_new
            h_new = sigmoid(gates[:, 2 * C : 3 * C]) * jnp.tanh(c_new)
            lines = [y + i for y, count in groups for i in range(count)]
            for i, line in enumerate(lines):
                inside = masks[width]
                if line < 0:
                    inside = inside & has_n
                if line >= CY:
                    inside = inside & has_s
                h_row = jnp.where(inside, h_new[i * width : (i + 1) * width, :], 0.0)
                begin = (line + TOP) * FW + 16
                edge = (width - WIDE) // 2
                hid[layer, t, begin - edge : begin + WIDE + edge, :] = h_row
                cell[layer, (line + TOP) * WIDE : (line + TOP + 1) * WIDE, :] = c_new[
                    i * width + edge : (i + 1) * width - edge, :
                ]
                for b in range(3):
                    zh[layer, t, b, (line + TOP) * WIDE : (line + TOP + 1) * WIDE, :] = hid[
                        layer, t, begin + b - 1 : begin + b - 1 + WIDE, :
                    ].astype(BF)

        return [functools.partial(chunk, groups) for groups in chunks or all_rows(layer, t)]

    begin = pl.multiple_of(core * (HALF * C), C)
    half = pl.ds(begin, HALF * C)

    def give(slot, src, dst):
        return pltpu.make_async_remote_copy(
            src_ref=src, dst_ref=dst, send_sem=o_send.at[slot], recv_sem=o_recv.at[slot],
            device_id=partner, device_id_type=MESH,
        )

    def give_hidden(t):
        return give(t, hs.at[t], out_h.at[0, t, 0, :, half])

    def give_cell():
        return give(TIME, cs, out_c.at[0, 0, :, half])

    def hidden_of(layer, t, x):
        return hid[layer, t, pl.ds(TOP * FW + 20 + x, CY, stride=FW), :].astype(BF)

    def cell_of(layer, x):
        return cell[layer, pl.ds(TOP * WIDE + 4 + x, CY, stride=WIDE), :]

    def put_hidden(layer, t):
        @pl.when(core == layer)
        def _():
            for x in range(HALF):
                out_h[0, t, 0, :, pl.ds(pl.multiple_of(begin + C * x, C), C)] = hidden_of(layer, t, x)

        @pl.when(core != layer)
        def _():
            for x in range(HALF):
                hs[t, :, C * x : C * (x + 1)] = hidden_of(layer, t, x)
            give_hidden(t).start()

    def put_cell(layer):
        @pl.when(core == layer)
        def _():
            for x in range(HALF):
                out_c[0, 0, :, pl.ds(pl.multiple_of(begin + C * x, C), C)] = cell_of(layer, x)

        @pl.when(core != layer)
        def _():
            for x in range(HALF):
                cs[:, C * x : C * (x + 1)] = cell_of(layer, x)
            give_cell().start()

    for p in range(2):
        own_w[p].wait()

    def get_weights(t):
        if t == 0:
            bias_copy().wait_recv()
            weight_copy(0).wait_recv()
        if t == 1:
            weight_copy(1).wait_recv()

    @pl.when(first_stage)
    def _():
        orders = (
            ([[(-3, 4)], [(1, 3)], [(4, 3)], [(7, 4)]], [[(-2, 4)], [(2, 4)], [(6, 4)]], "aabSabSabS", ((2,), (1, 0, 3), (4,))),
            ([[(-2, 4)], [(2, 4)], [(6, 4)]], [[(-1, 4)], [(3, 3)], [(6, 3)]], "aabSabSbS", ((1, 2), (3,), (0, 4))),
            ([[(-1, 4)], [(5, 4)], [(3, 2)]], [[(0, 2), (6, 2)], [(2, 4)]], "aabSabS", ((1, 0, 2, 3), (4,))),
        )
        for t in range(TIME):
            await_frame(t)
            get_weights(t)
            get_frame(t)
            lower, upper, order, kinds = orders[t]
            lower = iter(step(0, t, FIRST if t == 0 else WIDE, chunks=lower))
            upper = iter(step(1, t, chunks=upper))
            kinds = iter(kinds)
            copies = stage_copies(t)
            for what in order:
                if what == "a":
                    next(lower)()
                elif what == "b":
                    next(upper)()
                else:
                    for kind in next(kinds):
                        copies[kind].start()
        for t in range(TIME):
            for layer in range(2):
                put_hidden(layer, t)
        for layer in range(2):
            put_cell(layer)

    @pl.when(jnp.logical_not(first_stage))
    def _():
        for t in range(TIME):
            get_weights(t)
            if t > 0:
                hidden_part(0, t)
                hidden_part(1, t)
            get_hidden(t)
            for chunk in step(0, t, split=True):
                chunk()
            put_hidden(0, t)
            if t == TIME - 1:
                put_cell(0)
            for chunk in step(1, t, split=True):
                chunk()
            put_hidden(1, t)
        put_cell(1)

    bias_copy().wait_send()
    for p in range(2):
        weight_copy(p).wait_send()

    @pl.when(first_stage)
    def _():
        for t in range(TIME):
            for sends, _, cp in frame_copies(t):
                pl.when(sends)(cp.wait_send)
            for cp in stage_copies(t):
                cp.wait_send()

    for t in range(TIME):
        give_hidden(t).wait()
    give_cell().wait()


def local(frames, weights, bias):
    vmem = pl.BlockSpec(memory_space=pltpu.VMEM)
    hbm = pl.BlockSpec(memory_space=pltpu.HBM)
    dma = pltpu.SemaphoreType.DMA
    return pl.pallas_call(
        kernel,
        out_shape=(
            pltpu.VMEM((1, TIME, 1, CY, CX * C), BF),
            pltpu.VMEM((1, 1, CY, CX * C), F32),
        ),
        in_specs=[hbm, hbm, vmem],
        out_specs=(vmem, vmem),
        scratch_shapes=[
            pltpu.VMEM((TIME, CY, CX * C), BF),
            pltpu.VMEM((CY * CX, C), F32),
            pltpu.VMEM((TIME, CY, CX, C), BF),
            pltpu.VMEM((TIME, ROWS, FIRST, C), BF),
            pltpu.VMEM((TIME, (ROWS + 2) * WIDE, C), BF),
            pltpu.VMEM((TIME, ROWS * IW, C), F32),
            pltpu.VMEM((3, ROWS * FIRST, C), BF),
            pltpu.VMEM((TIME, 3, ROWS * WIDE, C), BF),
            pltpu.VMEM((2, TIME, 3, ROWS * WIDE, C), BF),
            pltpu.VMEM((2, TIME, ROWS * FW, C), F32),
            pltpu.VMEM((2, ROWS * WIDE, C), F32),
            pltpu.VMEM(((CY + 4) * WIDE, 4 * C), F32),
            pltpu.VMEM(((CY + 2) * WIDE, 4 * C), F32),
            pltpu.VMEM((2, 3, 3, 2 * C, 4 * C), BF),
            pltpu.VMEM((2, 8, 4 * C), F32),
            pltpu.VMEM((TIME, CY, HALF * C), BF),
            pltpu.VMEM((CY, HALF * C), F32),
            dma((12,)),
            dma((3,)),
            dma((3,)),
            dma((TIME, 5)),
            dma((TIME, 5)),
            dma((TIME, 5)),
            dma((TIME, 5)),
            dma((TIME + 1,)),
            dma((TIME + 1,)),
        ],
        compiler_params=pltpu.CompilerParams(
            collective_id=0, has_side_effects=True, vmem_limit_bytes=58 * 2**20
        ),
    )(frames, weights, bias)


def solution(mesh):
    return jax.shard_map(
        local,
        mesh=mesh,
        in_specs=(P(None, "tile", None, None), P("section", None, None, None, None), P("section", None)),
        out_specs=(P("section", None, "tile", None, None), P("section", "tile", None, None)),
        check_vma=False,
    )
```

```python
import functools

import jax
import jax.numpy as jnp
from jax import lax
from jax.experimental import pallas as pl
from jax.experimental.pallas import tpu as pltpu
from jax.sharding import PartitionSpec as P

MESH = pl.DeviceIdType.MESH
TCOLS = 8
TROWS = 8
C = 128
CX, CY, TIME = 80, 8, 3
HALF = CX // 2
TOP = 4
ROWS = CY + 2 * TOP
WIDE = 48
FIRST = 64
FW = 80
IW = 88
CHUNKS = ({14: (4, 3, 3, 4), 12: (4, 4, 4), 10: (4, 3, 3)}, {12: (6, 6), 10: (5, 5), 8: (4, 4)})
OWN = (((-2, 4), (2, 4), (6, 4)), ((-1, 4), (3, 3), (6, 3)), ((0, 2), (6, 2), (2, 4)))
BF, F32 = jnp.bfloat16, jnp.float32


def sigmoid(v):
    return 0.5 * jnp.tanh(0.5 * v) + 0.5


def kernel(
    frames, weights, bias, out_h, out_c,
    fr, s32, fyb, hb, hz, fin, zin0, zin, zh, hid, cell, part0, part1, wv, bv, hs, cs,
    local_sem, w_send, w_recv, fr_send, fr_recv, z_send, z_recv, o_send, o_recv,
):
    section, tile = lax.axis_index("section"), lax.axis_index("tile")
    stage, core = section // 2, section % 2
    first_stage = stage == 0
    row, col = tile // TCOLS, tile % TCOLS
    has_n, has_s = row > 0, row < TROWS - 1
    has_side = jnp.where(core == 0, col > 0, col < TCOLS - 1)
    side = 2 * core - 1
    partner = (2 * stage + 1 - core, tile)

    def at(stage_of, core_of, tile_of):
        return (2 * stage_of + core_of, tile_of)

    own_w = [
        pltpu.make_async_copy(
            weights.at[0, :, :, pl.ds(C * p, C), :], wv.at[core, :, :, pl.ds(C * p, C), :], local_sem.at[p]
        )
        for p in range(2)
    ]
    load_f = pltpu.make_async_copy(frames.at[:, 0], fr, local_sem.at[2])

    @pl.when(first_stage)
    def _():
        load_f.start()

    for cp in own_w:
        cp.start()

    def bias_copy():
        return pltpu.make_async_remote_copy(
            src_ref=bv.at[core], dst_ref=bv.at[core], send_sem=w_send.at[2], recv_sem=w_recv.at[2],
            device_id=partner, device_id_type=MESH,
        )

    def weight_copy(p):
        return pltpu.make_async_remote_copy(
            src_ref=weights.at[0, :, :, pl.ds(C * p, C), :], dst_ref=wv.at[core, :, :, pl.ds(C * p, C), :],
            send_sem=w_send.at[p], recv_sem=w_recv.at[p], device_id=partner, device_id_type=MESH,
        )

    cols48 = pl.multiple_of(32 * core, 16)
    to48 = pl.multiple_of(16 * (1 - core), 16)
    cols16 = pl.multiple_of(64 * core, 16)
    to16 = pl.multiple_of(48 * (1 - core), 16)

    def frame_copies(t):
        n = TOP - t

        def copy(kind, from_row, to_row, count, wide, target):
            src = fyb.at[t, pl.ds(from_row, count), pl.ds(cols48, WIDE) if wide else pl.ds(cols16, 16)]
            dst = hb.at[t, pl.ds(to_row, count), pl.ds(to48, WIDE) if wide else pl.ds(to16, 16)]
            return pltpu.make_async_remote_copy(
                src_ref=src, dst_ref=dst, send_sem=fr_send.at[t, kind], recv_sem=fr_recv.at[t, kind],
                device_id=target, device_id_type=MESH,
            )

        return [
            (has_side & has_s, has_side & has_n, copy(3, CY - n, TOP - n, n, False, at(0, 1 - core, tile + side + TCOLS))),
            (has_side & has_n, has_side & has_s, copy(4, 0, TOP + CY, n, False, at(0, 1 - core, tile + side - TCOLS))),
            (has_s, has_n, copy(0, CY - n, TOP - n, n, True, at(0, core, tile + TCOLS))),
            (has_n, has_s, copy(1, 0, TOP + CY, n, True, at(0, core, tile - TCOLS))),
            (has_side, has_side, copy(2, 0, TOP, CY, False, at(0, 1 - core, tile + side))),
        ]

    def stage_copies(t, receiving=False):
        k = TIME - 1 - t

        def copy(kind, from_row, to_row, count, target, lands=None):
            lands = kind if receiving or lands is None else lands
            return pltpu.make_async_remote_copy(
                src_ref=zh.at[1, t, 1, pl.ds((TOP + from_row) * WIDE, count * WIDE)],
                dst_ref=hz.at[t, pl.ds(pl.multiple_of((TOP + to_row) * WIDE, WIDE), count * WIDE)],
                send_sem=z_send.at[t, kind], recv_sem=z_recv.at[t, lands], device_id=target, device_id_type=MESH,
            )

        unread = CY + TOP
        return [
            copy(
                0, CY - 2 - k, jnp.where(has_s, -2 - k, unread), 2, at(1, core, jnp.where(has_s, tile + TCOLS, tile)),
                jnp.where(has_s, 0, 1),
            ),
            copy(
                1, k, jnp.where(has_n, CY + k, unread), 2, at(1, core, jnp.where(has_n, tile - TCOLS, tile)),
                jnp.where(has_n, 1, 0),
            ),
            *[copy(2 + i, y, y, count, at(1, core, tile)) for i, (y, count) in enumerate(OWN[t])],
        ]

    def put_input(t, rows, width, first_column, low=0, count=None):
        target = zin0 if width == FIRST else zin.at[t]
        count = width if count is None else count
        for y in rows:
            for b in range(3):
                begin = y * IW + first_column + low + b - 1
                target[b, y * width + low : y * width + low + count, :] = fin[t, begin : begin + count, :].astype(BF)

    def frame_width(t):
        return (FIRST, 12) if t == 0 else (WIDE, 20)

    own_rows = range(TOP, TOP + CY)

    def await_frame(t):
        for _, gets, cp in frame_copies(t):
            pl.when(gets)(cp.wait_recv)

    def get_frame(t):
        halo_rows = [*range(t, TOP), *range(TOP + CY, ROWS - t)]
        width, first_column = frame_width(t)
        for y in halo_rows:
            fin[t, pl.ds(pl.multiple_of(y * IW + 8 + 8 * core, 8), FIRST), :] = hb[t, y].astype(F32)
        for y in own_rows:
            fin[t, pl.ds(pl.multiple_of(y * IW + 8 + 56 * core, 8), 16), :] = hb[
                t, y, pl.ds(pl.multiple_of(48 * core, 16), 16), :
            ].astype(F32)
        put_input(t, halo_rows, width, first_column)
        put_input(t, own_rows, width, first_column, 0, 16)
        put_input(t, own_rows, width, first_column, width - 16, 16)

    def get_hidden(t, pieces):
        k = TIME - 1 - t
        copies = stage_copies(t, receiving=True)
        parts = [(copies[2 + i : 3 + i], range(y, y + count)) for i, (y, count) in enumerate(OWN[t])]
        parts.append((copies[:2], [-2 - k, -1 - k, CY + k, CY + k + 1]))
        for piece in pieces:
            waits, lines = parts[piece]
            for cp in waits:
                cp.wait_recv()
            rows = [TOP + line for line in lines]
            for y in rows:
                fin[t, y * IW + 24 : y * IW + 24 + WIDE, :] = hz[t, y * WIDE : (y + 1) * WIDE, :].astype(F32)
            put_input(t, rows, WIDE, 24)

    @pl.when(first_stage)
    def _():
        @pl.when(jnp.logical_not(has_n & has_s & has_side))
        def _():
            hb[...] = jnp.zeros_like(hb)

    @pl.when(jnp.logical_not(first_stage))
    def _():
        hz[...] = jnp.zeros_like(hz)

    barrier = pltpu.get_barrier_semaphore()

    def greet(device):
        pl.semaphore_signal(barrier, inc=1, device_id=device, device_id_type=MESH)

    @pl.when(first_stage)
    def _():
        pl.when(has_side & has_n)(lambda: greet(at(0, 1 - core, tile + side - TCOLS)))
        pl.when(has_side & has_s)(lambda: greet(at(0, 1 - core, tile + side + TCOLS)))
        pl.when(has_side)(lambda: greet(at(0, 1 - core, tile + side)))
        pl.when(has_n)(lambda: greet(at(0, core, tile - TCOLS)))
        pl.when(has_s)(lambda: greet(at(0, core, tile + TCOLS)))

    pl.when(has_n)(lambda: greet(at(1 - stage, core, tile - TCOLS)))
    pl.when(has_s)(lambda: greet(at(1 - stage, core, tile + TCOLS)))
    greet(at(1 - stage, core, tile))
    greet(partner)

    def put_rows(t):
        for x in range(CX):
            s32[CY * x : CY * (x + 1), :] = fr[t, :, C * x : C * (x + 1)].astype(F32)
        for y in range(CY):
            fyb[t, y] = s32[pl.ds(y, CX, stride=CY), :].astype(BF)

    def send_frame(t):
        for sends, _, cp in frame_copies(t):
            pl.when(sends)(cp.start)

    bv[core] = jnp.broadcast_to(bias[...].astype(F32), (8, 4 * C))

    @pl.when(first_stage)
    def _():
        load_f.wait()
        put_rows(0)

    one = lambda c: c.astype(jnp.int32)
    near = one(has_n) + one(has_s)
    mine = 2 + near
    tiles = near + one(has_side) + one(has_side & has_n) + one(has_side & has_s)
    pl.semaphore_wait(barrier, mine + jnp.where(first_stage, tiles, 0))

    @pl.when(first_stage)
    def _():
        send_frame(0)

    bias_copy().start()
    weight_copy(0).start()

    @pl.when(first_stage)
    def _():
        put_rows(1)
        send_frame(1)
        put_rows(2)
        send_frame(2)

    weight_copy(1).start()

    hid[...] = jnp.zeros_like(hid)
    fin[...] = jnp.zeros_like(fin)

    @pl.when(first_stage)
    def _():
        for t in range(TIME):
            for y in range(CY):
                fin[t, pl.ds(pl.multiple_of((y + TOP) * IW + 24 - 8 * core, 8), WIDE), :] = fyb[
                    t, y, pl.ds(cols48, WIDE), :
                ].astype(F32)
            width, first_column = frame_width(t)
            put_input(t, own_rows, width, first_column, 16, width - 32)

    def column_mask(width, first):
        x = lax.broadcasted_iota(jnp.int32, (width, C), 0) + (first + HALF * core + CX * col)
        return (x >= 0) & (x < CX * TCOLS)

    masks = {WIDE: column_mask(WIDE, -4), FIRST: column_mask(FIRST, -12)}

    def taps(groups, width, array):
        pieces = []
        for a in range(3):
            for b in range(3):
                rows = [array[b, pl.ds((y + a - 1 + TOP) * width, count * width), :] for y, count in groups]
                pieces.append(rows[0] if len(rows) == 1 else jnp.concatenate(rows, axis=0))
        return jnp.concatenate(pieces, axis=1)

    def all_rows(layer, t):
        y = -((1 - layer) + (TIME - 1 - t))
        chunks = []
        for count in CHUNKS[layer][CY - 2 * y]:
            chunks.append([(y, count)])
            y += count
        return chunks

    parts = (part0, part1)

    def hidden_part(layer, t):
        k = (1 - layer) + (TIME - 1 - t)
        for groups in all_rows(layer, t):
            ((y, count),) = groups
            parts[layer][(y + k) * WIDE : (y + k + count) * WIDE, :] = jnp.dot(
                taps(groups, WIDE, zh.at[layer, t - 1]),
                wv[layer, :, :, C:, :].reshape(9 * C, 4 * C),
                preferred_element_type=F32,
            )

    def step(layer, t, width=WIDE, split=False, chunks=None):
        k = (1 - layer) + (TIME - 1 - t)
        split = split and t > 0
        whole = t > 0 and not split
        source = zh.at[0, t] if layer == 1 else (zin0 if width == FIRST else zin.at[t])

        def chunk(groups):
            columns = taps(groups, width, source)
            factors = wv[layer, :, :, :C, :].reshape(9 * C, 4 * C)
            if whole:
                columns = jnp.concatenate([taps(groups, width, zh.at[layer, t - 1]), columns], axis=1)
                factors = jnp.concatenate([wv[layer, :, :, C:, :].reshape(9 * C, 4 * C), factors], axis=0)
            gates = jnp.dot(columns, factors, preferred_element_type=F32) + bv[layer, 0:1, :]
            if split:
                gates = gates + parts[layer][(groups[0][0] + k) * WIDE : (groups[0][0] + k + groups[0][1]) * WIDE, :]
            c_new = sigmoid(gates[:, :C]) * jnp.tanh(gates[:, 3 * C :])
            if t > 0:
                old = [cell[layer, pl.ds((y + TOP) * WIDE, count * WIDE), :] for y, count in groups]
                old = old[0] if len(old) == 1 else jnp.concatenate(old, axis=0)
                c_new = sigmoid(gates[:, C : 2 * C]) * old + c_new
            h_new = sigmoid(gates[:, 2 * C : 3 * C]) * jnp.tanh(c_new)
            lines = [y + i for y, count in groups for i in range(count)]
            for i, line in enumerate(lines):
                inside = masks[width]
                if line < 0:
                    inside = inside & has_n
                if line >= CY:
                    inside = inside & has_s
                h_row = jnp.where(inside, h_new[i * width : (i + 1) * width, :], 0.0)
                begin = (line + TOP) * FW + 16
                edge = (width - WIDE) // 2
                hid[layer, t, begin - edge : begin + WIDE + edge, :] = h_row
                cell[layer, (line + TOP) * WIDE : (line + TOP + 1) * WIDE, :] = c_new[
                    i * width + edge : (i + 1) * width - edge, :
                ]
                for b in range(3):
                    zh[layer, t, b, (line + TOP) * WIDE : (line + TOP + 1) * WIDE, :] = hid[
                        layer, t, begin + b - 1 : begin + b - 1 + WIDE, :
                    ].astype(BF)

        return [functools.partial(chunk, groups) for groups in chunks or all_rows(layer, t)]

    half = pl.ds(pl.multiple_of(core * (HALF * C), C), HALF * C)

    def keep(slot, src, dst):
        return pltpu.make_async_copy(src.at[core], dst, local_sem.at[8 + slot])

    def give(slot, src, dst):
        return pltpu.make_async_remote_copy(
            src_ref=src.at[1 - core], dst_ref=dst, send_sem=o_send.at[slot], recv_sem=o_recv.at[slot],
            device_id=partner, device_id_type=MESH,
        )

    def hidden_result(t):
        return t, hs.at[:, t], out_h.at[0, t, 0, :, half]

    cell_result = TIME, cs, out_c.at[0, 0, :, half]

    def put_hidden(layer, t):
        for x in range(HALF):
            hs[layer, t, :, C * x : C * (x + 1)] = hid[
                layer, t, pl.ds(TOP * FW + 20 + x, CY, stride=FW), :
            ].astype(BF)

    def put_cell(layer):
        for x in range(HALF):
            cs[layer, :, C * x : C * (x + 1)] = cell[layer, pl.ds(TOP * WIDE + 4 + x, CY, stride=WIDE), :]

    for p in range(2):
        own_w[p].wait()

    def get_weights(t):
        if t == 0:
            bias_copy().wait_recv()
            weight_copy(0).wait_recv()
        if t == 1:
            weight_copy(1).wait_recv()

    @pl.when(first_stage)
    def _():
        orders = (
            ([[(-3, 4)], [(1, 3)], [(4, 3)], [(7, 4)]], [[(-2, 4)], [(2, 4)], [(6, 4)]], "aabSabSabS", ((2,), (1, 0, 3), (4,))),
            ([[(0, 4)], [(4, 4)], [(-2, 2), (8, 2)]], [[(1, 2), (5, 2)], [(-1, 2), (3, 2), (7, 2)]], "aabSabS", ((1, 0), (2, 3, 4))),
            ([[(-1, 4)], [(5, 4)], [(3, 2)]], [[(0, 2), (6, 2)], [(2, 4)]], "aabSabS", ((1, 0, 2, 3), (4,))),
        )
        for t in range(TIME):
            await_frame(t)
            get_weights(t)
            get_frame(t)
            lower, upper, order, kinds = orders[t]
            lower = iter(step(0, t, FIRST if t == 0 else WIDE, chunks=lower))
            upper = iter(step(1, t, chunks=upper))
            kinds = iter(kinds)
            copies = stage_copies(t)
            for what in order:
                if what == "a":
                    next(lower)()
                elif what == "b":
                    next(upper)()
                else:
                    for kind in next(kinds):
                        copies[kind].start()
        for t in range(TIME):
            for layer in range(2):
                put_hidden(layer, t)
            give(*hidden_result(t)).start()
            keep(*hidden_result(t)).start()
        for layer in range(2):
            put_cell(layer)
        give(*cell_result).start()
        keep(*cell_result).start()

    @pl.when(jnp.logical_not(first_stage))
    def _():
        for t in range(TIME):
            get_weights(t)
            if t == 0:
                get_hidden(0, (0, 1))
                chunks = iter(step(0, 0, chunks=[[(1, 3)], [(4, 3)], [(-3, 4)], [(7, 4)]]))
                next(chunks)()
                get_hidden(0, (2,))
                next(chunks)()
                get_hidden(0, (3,))
            else:
                hidden_part(0, t)
                hidden_part(1, t)
                get_hidden(t, (0, 1, 2, 3))
                chunks = step(0, t, split=True)
            for chunk in chunks:
                chunk()
            if t < TIME - 1:
                for chunk in step(1, t, split=True):
                    chunk()
                put_hidden(0, t)
                put_hidden(1, t)
                give(*hidden_result(t)).start()
                keep(*hidden_result(t)).start()
        t = TIME - 1
        upper, lower = step(1, t, split=True)
        upper()
        put_hidden(0, t)
        put_cell(0)
        for result in (hidden_result(t), cell_result):
            pl.when(core == 1)(give(*result).start)
            pl.when(core == 0)(keep(*result).start)
        lower()
        put_hidden(1, t)
        put_cell(1)
        for result in (hidden_result(t), cell_result):
            pl.when(core == 0)(give(*result).start)
            pl.when(core == 1)(keep(*result).start)

    bias_copy().wait_send()
    for p in range(2):
        weight_copy(p).wait_send()

    @pl.when(first_stage)
    def _():
        for t in range(TIME):
            for sends, _, cp in frame_copies(t):
                pl.when(sends)(cp.wait_send)
            for cp in stage_copies(t):
                cp.wait_send()

    for result in (*[hidden_result(t) for t in range(TIME)], cell_result):
        keep(*result).wait()
        give(*result).wait()


def local(frames, weights, bias):
    vmem = pl.BlockSpec(memory_space=pltpu.VMEM)
    hbm = pl.BlockSpec(memory_space=pltpu.HBM)
    dma = pltpu.SemaphoreType.DMA
    return pl.pallas_call(
        kernel,
        out_shape=(
            pltpu.VMEM((1, TIME, 1, CY, CX * C), BF),
            pltpu.VMEM((1, 1, CY, CX * C), F32),
        ),
        in_specs=[hbm, hbm, vmem],
        out_specs=(vmem, vmem),
        scratch_shapes=[
            pltpu.VMEM((TIME, CY, CX * C), BF),
            pltpu.VMEM((CY * CX, C), F32),
            pltpu.VMEM((TIME, CY, CX, C), BF),
            pltpu.VMEM((TIME, ROWS, FIRST, C), BF),
            pltpu.VMEM((TIME, (ROWS + 2) * WIDE, C), BF),
            pltpu.VMEM((TIME, ROWS * IW, C), F32),
            pltpu.VMEM((3, ROWS * FIRST, C), BF),
            pltpu.VMEM((TIME, 3, ROWS * WIDE, C), BF),
            pltpu.VMEM((2, TIME, 3, ROWS * WIDE, C), BF),
            pltpu.VMEM((2, TIME, ROWS * FW, C), F32),
            pltpu.VMEM((2, ROWS * WIDE, C), F32),
            pltpu.VMEM(((CY + 4) * WIDE, 4 * C), F32),
            pltpu.VMEM(((CY + 2) * WIDE, 4 * C), F32),
            pltpu.VMEM((2, 3, 3, 2 * C, 4 * C), BF),
            pltpu.VMEM((2, 8, 4 * C), F32),
            pltpu.VMEM((2, TIME, CY, HALF * C), BF),
            pltpu.VMEM((2, CY, HALF * C), F32),
            dma((12,)),
            dma((3,)),
            dma((3,)),
            dma((TIME, 5)),
            dma((TIME, 5)),
            dma((TIME, 5)),
            dma((TIME, 5)),
            dma((TIME + 1,)),
            dma((TIME + 1,)),
        ],
        compiler_params=pltpu.CompilerParams(
            collective_id=0, has_side_effects=True, vmem_limit_bytes=58 * 2**20
        ),
    )(frames, weights, bias)


def solution(mesh):
    return jax.shard_map(
        local,
        mesh=mesh,
        in_specs=(P(None, "tile", None, None), P("section", None, None, None, None), P("section", None)),
        out_specs=(P("section", None, "tile", None, None), P("section", "tile", None, None)),
        check_vma=False,
    )
```

```python
import functools

import jax
import jax.numpy as jnp
from jax import lax
from jax.experimental import pallas as pl
from jax.experimental.pallas import tpu as pltpu
from jax.sharding import PartitionSpec as P

MESH = pl.DeviceIdType.MESH
TCOLS = 8
TROWS = 8
C = 128
CX, CY, TIME = 80, 8, 3
HALF = CX // 2
TOP = 4
ROWS = CY + 2 * TOP
WIDE = 48
FIRST = 64
FW = 80
IW = 88
CHUNKS = ({14: (4, 3, 3, 4), 12: (4, 4, 4), 10: (4, 3, 3)}, {12: (6, 6), 10: (5, 5), 8: (4, 4)})
OWN = (((-2, 4), (2, 4), (6, 4)), ((-1, 4), (3, 3), (6, 3)), ((0, 2), (6, 2), (2, 4)))
BF, F32 = jnp.bfloat16, jnp.float32


def sigmoid(v):
    return 0.5 * jnp.tanh(0.5 * v) + 0.5


def kernel(
    frames, weights, bias, out_h, out_c,
    fr, s32, fyb, hb, hz, fin, zin0, zin, zh, hid, cell, part0, part1, wv, bv, hs, cs,
    local_sem, w_send, w_recv, fr_send, fr_recv, z_send, z_recv, o_send, o_recv,
):
    section, tile = lax.axis_index("section"), lax.axis_index("tile")
    stage, core = section // 2, section % 2
    first_stage = stage == 0
    row, col = tile // TCOLS, tile % TCOLS
    has_n, has_s = row > 0, row < TROWS - 1
    has_side = jnp.where(core == 0, col > 0, col < TCOLS - 1)
    side = 2 * core - 1
    partner = (2 * stage + 1 - core, tile)

    def at(stage_of, core_of, tile_of):
        return (2 * stage_of + core_of, tile_of)

    own_w = [
        pltpu.make_async_copy(
            weights.at[0, :, :, pl.ds(C * p, C), :], wv.at[core, :, :, pl.ds(C * p, C), :], local_sem.at[p]
        )
        for p in range(2)
    ]
    load_f = pltpu.make_async_copy(frames.at[:, 0], fr, local_sem.at[2])

    @pl.when(first_stage)
    def _():
        load_f.start()

    for cp in own_w:
        cp.start()

    def bias_copy():
        return pltpu.make_async_remote_copy(
            src_ref=bv.at[core], dst_ref=bv.at[core], send_sem=w_send.at[2], recv_sem=w_recv.at[2],
            device_id=partner, device_id_type=MESH,
        )

    def weight_copy(p):
        return pltpu.make_async_remote_copy(
            src_ref=weights.at[0, :, :, pl.ds(C * p, C), :], dst_ref=wv.at[core, :, :, pl.ds(C * p, C), :],
            send_sem=w_send.at[p], recv_sem=w_recv.at[p], device_id=partner, device_id_type=MESH,
        )

    cols48 = pl.multiple_of(32 * core, 16)
    to48 = pl.multiple_of(16 * (1 - core), 16)
    cols16 = pl.multiple_of(64 * core, 16)
    to16 = pl.multiple_of(48 * (1 - core), 16)

    def frame_copies(t):
        n = TOP - t

        def copy(kind, from_row, to_row, count, wide, target):
            src = fyb.at[t, pl.ds(from_row, count), pl.ds(cols48, WIDE) if wide else pl.ds(cols16, 16)]
            dst = hb.at[t, pl.ds(to_row, count), pl.ds(to48, WIDE) if wide else pl.ds(to16, 16)]
            return pltpu.make_async_remote_copy(
                src_ref=src, dst_ref=dst, send_sem=fr_send.at[t, kind], recv_sem=fr_recv.at[t, kind],
                device_id=target, device_id_type=MESH,
            )

        return [
            (has_side & has_s, has_side & has_n, copy(3, CY - n, TOP - n, n, False, at(0, 1 - core, tile + side + TCOLS))),
            (has_side & has_n, has_side & has_s, copy(4, 0, TOP + CY, n, False, at(0, 1 - core, tile + side - TCOLS))),
            (has_side, has_side, copy(2, 0, TOP, CY, False, at(0, 1 - core, tile + side))),
            (has_s, has_n, copy(0, CY - n, TOP - n, n, True, at(0, core, tile + TCOLS))),
            (has_n, has_s, copy(1, 0, TOP + CY, n, True, at(0, core, tile - TCOLS))),
        ]

    def stage_copies(t, receiving=False):
        k = TIME - 1 - t

        def copy(kind, from_row, to_row, count, target, lands=None):
            lands = kind if receiving or lands is None else lands
            return pltpu.make_async_remote_copy(
                src_ref=zh.at[1, t, 1, pl.ds((TOP + from_row) * WIDE, count * WIDE)],
                dst_ref=hz.at[t, pl.ds(pl.multiple_of((TOP + to_row) * WIDE, WIDE), count * WIDE)],
                send_sem=z_send.at[t, kind], recv_sem=z_recv.at[t, lands], device_id=target, device_id_type=MESH,
            )

        unread = CY + TOP
        return [
            copy(
                0, CY - 2 - k, jnp.where(has_s, -2 - k, unread), 2, at(1, core, jnp.where(has_s, tile + TCOLS, tile)),
                jnp.where(has_s, 0, 1),
            ),
            copy(
                1, k, jnp.where(has_n, CY + k, unread), 2, at(1, core, jnp.where(has_n, tile - TCOLS, tile)),
                jnp.where(has_n, 1, 0),
            ),
            *[copy(2 + i, y, y, count, at(1, core, tile)) for i, (y, count) in enumerate(OWN[t])],
        ]

    def put_input(t, rows, width, first_column, low=0, count=None):
        target = zin0 if width == FIRST else zin.at[t]
        count = width if count is None else count
        for y in rows:
            for b in range(3):
                begin = y * IW + first_column + low + b - 1
                target[b, y * width + low : y * width + low + count, :] = fin[t, begin : begin + count, :].astype(BF)

    def frame_width(t):
        return (FIRST, 12) if t == 0 else (WIDE, 20)

    own_rows = range(TOP, TOP + CY)

    def get_side(t):
        _, gets, cp = frame_copies(t)[2]
        pl.when(gets)(cp.wait_recv)
        width, first_column = frame_width(t)
        for y in own_rows:
            fin[t, pl.ds(pl.multiple_of(y * IW + 8 + 56 * core, 8), 16), :] = hb[
                t, y, pl.ds(pl.multiple_of(48 * core, 16), 16), :
            ].astype(F32)
        put_input(t, own_rows, width, first_column, 0, 16)
        put_input(t, own_rows, width, first_column, width - 16, 16)

    def get_rows(t):
        copies = frame_copies(t)
        for _, gets, cp in copies[:2] + copies[3:]:
            pl.when(gets)(cp.wait_recv)
        halo_rows = [*range(t, TOP), *range(TOP + CY, ROWS - t)]
        width, first_column = frame_width(t)
        for y in halo_rows:
            fin[t, pl.ds(pl.multiple_of(y * IW + 8 + 8 * core, 8), FIRST), :] = hb[t, y].astype(F32)
        put_input(t, halo_rows, width, first_column)

    def get_hidden(t, pieces):
        k = TIME - 1 - t
        copies = stage_copies(t, receiving=True)
        parts = [(copies[2 + i : 3 + i], range(y, y + count)) for i, (y, count) in enumerate(OWN[t])]
        parts.append((copies[:2], [-2 - k, -1 - k, CY + k, CY + k + 1]))
        for piece in pieces:
            waits, lines = parts[piece]
            for cp in waits:
                cp.wait_recv()
            rows = [TOP + line for line in lines]
            for y in rows:
                fin[t, y * IW + 24 : y * IW + 24 + WIDE, :] = hz[t, y * WIDE : (y + 1) * WIDE, :].astype(F32)
            put_input(t, rows, WIDE, 24)

    @pl.when(first_stage)
    def _():
        @pl.when(jnp.logical_not(has_n & has_s & has_side))
        def _():
            hb[...] = jnp.zeros_like(hb)

    @pl.when(jnp.logical_not(first_stage))
    def _():
        hz[...] = jnp.zeros_like(hz)

    barrier = pltpu.get_barrier_semaphore()

    def greet(device):
        pl.semaphore_signal(barrier, inc=1, device_id=device, device_id_type=MESH)

    @pl.when(first_stage)
    def _():
        pl.when(has_side & has_n)(lambda: greet(at(0, 1 - core, tile + side - TCOLS)))
        pl.when(has_side & has_s)(lambda: greet(at(0, 1 - core, tile + side + TCOLS)))
        pl.when(has_side)(lambda: greet(at(0, 1 - core, tile + side)))
        pl.when(has_n)(lambda: greet(at(0, core, tile - TCOLS)))
        pl.when(has_s)(lambda: greet(at(0, core, tile + TCOLS)))

    pl.when(has_n)(lambda: greet(at(1 - stage, core, tile - TCOLS)))
    pl.when(has_s)(lambda: greet(at(1 - stage, core, tile + TCOLS)))
    greet(at(1 - stage, core, tile))
    greet(partner)

    def put_rows(t):
        for x in range(CX):
            s32[CY * x : CY * (x + 1), :] = fr[t, :, C * x : C * (x + 1)].astype(F32)
        for y in range(CY):
            fyb[t, y] = s32[pl.ds(y, CX, stride=CY), :].astype(BF)

    def send_frame(t):
        for sends, _, cp in frame_copies(t):
            pl.when(sends)(cp.start)

    bv[core] = jnp.broadcast_to(bias[...].astype(F32), (8, 4 * C))

    @pl.when(first_stage)
    def _():
        load_f.wait()
        put_rows(0)

    one = lambda c: c.astype(jnp.int32)
    near = one(has_n) + one(has_s)
    mine = 2 + near
    tiles = near + one(has_side) + one(has_side & has_n) + one(has_side & has_s)
    pl.semaphore_wait(barrier, mine + jnp.where(first_stage, tiles, 0))

    @pl.when(first_stage)
    def _():
        send_frame(0)

    bias_copy().start()
    weight_copy(0).start()

    @pl.when(first_stage)
    def _():
        put_rows(1)
        send_frame(1)
        put_rows(2)
        send_frame(2)

    weight_copy(1).start()

    hid[...] = jnp.zeros_like(hid)
    fin[...] = jnp.zeros_like(fin)

    @pl.when(first_stage)
    def _():
        for t in range(TIME):
            for y in range(CY):
                fin[t, pl.ds(pl.multiple_of((y + TOP) * IW + 24 - 8 * core, 8), WIDE), :] = fyb[
                    t, y, pl.ds(cols48, WIDE), :
                ].astype(F32)
            width, first_column = frame_width(t)
            put_input(t, own_rows, width, first_column, 16, width - 32)

    def column_mask(width, first):
        x = lax.broadcasted_iota(jnp.int32, (width, C), 0) + (first + HALF * core + CX * col)
        return (x >= 0) & (x < CX * TCOLS)

    masks = {WIDE: column_mask(WIDE, -4), FIRST: column_mask(FIRST, -12)}

    def taps(groups, width, array):
        pieces = []
        for a in range(3):
            for b in range(3):
                rows = [array[b, pl.ds((y + a - 1 + TOP) * width, count * width), :] for y, count in groups]
                pieces.append(rows[0] if len(rows) == 1 else jnp.concatenate(rows, axis=0))
        return jnp.concatenate(pieces, axis=1)

    def all_rows(layer, t):
        y = -((1 - layer) + (TIME - 1 - t))
        chunks = []
        for count in CHUNKS[layer][CY - 2 * y]:
            chunks.append([(y, count)])
            y += count
        return chunks

    parts = (part0, part1)

    def hidden_part(layer, t):
        k = (1 - layer) + (TIME - 1 - t)
        for groups in all_rows(layer, t):
            ((y, count),) = groups
            parts[layer][(y + k) * WIDE : (y + k + count) * WIDE, :] = jnp.dot(
                taps(groups, WIDE, zh.at[layer, t - 1]),
                wv[layer, :, :, C:, :].reshape(9 * C, 4 * C),
                preferred_element_type=F32,
            )

    def step(layer, t, width=WIDE, split=False, chunks=None):
        k = (1 - layer) + (TIME - 1 - t)
        split = split and t > 0
        whole = t > 0 and not split
        source = zh.at[0, t] if layer == 1 else (zin0 if width == FIRST else zin.at[t])

        def chunk(groups):
            columns = taps(groups, width, source)
            factors = wv[layer, :, :, :C, :].reshape(9 * C, 4 * C)
            if whole:
                columns = jnp.concatenate([taps(groups, width, zh.at[layer, t - 1]), columns], axis=1)
                factors = jnp.concatenate([wv[layer, :, :, C:, :].reshape(9 * C, 4 * C), factors], axis=0)
            gates = jnp.dot(columns, factors, preferred_element_type=F32) + bv[layer, 0:1, :]
            if split:
                gates = gates + parts[layer][(groups[0][0] + k) * WIDE : (groups[0][0] + k + groups[0][1]) * WIDE, :]
            c_new = sigmoid(gates[:, :C]) * jnp.tanh(gates[:, 3 * C :])
            if t > 0:
                old = [cell[layer, pl.ds((y + TOP) * WIDE, count * WIDE), :] for y, count in groups]
                old = old[0] if len(old) == 1 else jnp.concatenate(old, axis=0)
                c_new = sigmoid(gates[:, C : 2 * C]) * old + c_new
            h_new = sigmoid(gates[:, 2 * C : 3 * C]) * jnp.tanh(c_new)
            lines = [y + i for y, count in groups for i in range(count)]
            for i, line in enumerate(lines):
                inside = masks[width]
                if line < 0:
                    inside = inside & has_n
                if line >= CY:
                    inside = inside & has_s
                h_row = jnp.where(inside, h_new[i * width : (i + 1) * width, :], 0.0)
                begin = (line + TOP) * FW + 16
                edge = (width - WIDE) // 2
                hid[layer, t, begin - edge : begin + WIDE + edge, :] = h_row
                cell[layer, (line + TOP) * WIDE : (line + TOP + 1) * WIDE, :] = c_new[
                    i * width + edge : (i + 1) * width - edge, :
                ]
                for b in range(3):
                    zh[layer, t, b, (line + TOP) * WIDE : (line + TOP + 1) * WIDE, :] = hid[
                        layer, t, begin + b - 1 : begin + b - 1 + WIDE, :
                    ].astype(BF)

        return [functools.partial(chunk, groups) for groups in chunks or all_rows(layer, t)]

    half = pl.ds(pl.multiple_of(core * (HALF * C), C), HALF * C)

    def keep(slot, src, dst):
        return pltpu.make_async_copy(src.at[core], dst, local_sem.at[8 + slot])

    def give(slot, src, dst):
        return pltpu.make_async_remote_copy(
            src_ref=src.at[1 - core], dst_ref=dst, send_sem=o_send.at[slot], recv_sem=o_recv.at[slot],
            device_id=partner, device_id_type=MESH,
        )

    def hidden_result(t):
        return t, hs.at[:, t], out_h.at[0, t, 0, :, half]

    cell_result = TIME, cs, out_c.at[0, 0, :, half]

    def put_hidden(layer, t):
        for x in range(HALF):
            hs[layer, t, :, C * x : C * (x + 1)] = hid[
                layer, t, pl.ds(TOP * FW + 20 + x, CY, stride=FW), :
            ].astype(BF)

    def put_cell(layer):
        for x in range(HALF):
            cs[layer, :, C * x : C * (x + 1)] = cell[layer, pl.ds(TOP * WIDE + 4 + x, CY, stride=WIDE), :]

    for p in range(2):
        own_w[p].wait()

    def get_weights(t):
        if t == 0:
            bias_copy().wait_recv()
            weight_copy(0).wait_recv()
        if t == 1:
            weight_copy(1).wait_recv()

    @pl.when(first_stage)
    def _():
        orders = (
            ([[(1, 3)], [(4, 3)], [(-3, 4)], [(7, 4)]], [[(2, 4)], [(-2, 4)], [(6, 4)]], "aabSRaabSbS", ((1, 0, 3), (2,), (4,))),
            ([[(0, 4)], [(4, 4)], [(-2, 2), (8, 2)]], [[(1, 2), (5, 2)], [(-1, 2), (3, 2), (7, 2)]], "RaabSabS", ((1, 0), (2, 3, 4))),
            ([[(-1, 4)], [(5, 4)], [(3, 2)]], [[(0, 2), (6, 2)], [(2, 4)]], "RaabSabS", ((1, 0, 2, 3), (4,))),
        )
        for t in range(TIME):
            get_weights(t)
            get_side(t)
            lower, upper, order, kinds = orders[t]
            lower = iter(step(0, t, FIRST if t == 0 else WIDE, chunks=lower))
            upper = iter(step(1, t, chunks=upper))
            kinds = iter(kinds)
            copies = stage_copies(t)
            for what in order:
                if what == "a":
                    next(lower)()
                elif what == "b":
                    next(upper)()
                elif what == "R":
                    get_rows(t)
                else:
                    for kind in next(kinds):
                        copies[kind].start()
        for t in range(TIME):
            for layer in range(2):
                put_hidden(layer, t)
            give(*hidden_result(t)).start()
            keep(*hidden_result(t)).start()
        for layer in range(2):
            put_cell(layer)
        give(*cell_result).start()
        keep(*cell_result).start()

    @pl.when(jnp.logical_not(first_stage))
    def _():
        for t in range(TIME):
            get_weights(t)
            if t == 0:
                get_hidden(0, (0, 1))
                chunks = iter(step(0, 0, chunks=[[(1, 3)], [(4, 3)], [(-3, 4)], [(7, 4)]]))
                next(chunks)()
                get_hidden(0, (2,))
                next(chunks)()
                get_hidden(0, (3,))
            else:
                hidden_part(0, t)
                hidden_part(1, t)
                get_hidden(t, (0, 1, 2, 3))
                chunks = step(0, t, split=True)
            for chunk in chunks:
                chunk()
            if t < TIME - 1:
                for chunk in step(1, t, split=True):
                    chunk()
                put_hidden(0, t)
                put_hidden(1, t)
                give(*hidden_result(t)).start()
                keep(*hidden_result(t)).start()
        t = TIME - 1
        upper, lower = step(1, t, split=True)
        upper()
        put_hidden(0, t)
        put_cell(0)
        for result in (hidden_result(t), cell_result):
            pl.when(core == 1)(give(*result).start)
            pl.when(core == 0)(keep(*result).start)
        lower()
        put_hidden(1, t)
        put_cell(1)
        for result in (hidden_result(t), cell_result):
            pl.when(core == 0)(give(*result).start)
            pl.when(core == 1)(keep(*result).start)

    bias_copy().wait_send()
    for p in range(2):
        weight_copy(p).wait_send()

    @pl.when(first_stage)
    def _():
        for t in range(TIME):
            for sends, _, cp in frame_copies(t):
                pl.when(sends)(cp.wait_send)
            for cp in stage_copies(t):
                cp.wait_send()

    for result in (*[hidden_result(t) for t in range(TIME)], cell_result):
        keep(*result).wait()
        give(*result).wait()


def local(frames, weights, bias):
    vmem = pl.BlockSpec(memory_space=pltpu.VMEM)
    hbm = pl.BlockSpec(memory_space=pltpu.HBM)
    dma = pltpu.SemaphoreType.DMA
    return pl.pallas_call(
        kernel,
        out_shape=(
            pltpu.VMEM((1, TIME, 1, CY, CX * C), BF),
            pltpu.VMEM((1, 1, CY, CX * C), F32),
        ),
        in_specs=[hbm, hbm, vmem],
        out_specs=(vmem, vmem),
        scratch_shapes=[
            pltpu.VMEM((TIME, CY, CX * C), BF),
            pltpu.VMEM((CY * CX, C), F32),
            pltpu.VMEM((TIME, CY, CX, C), BF),
            pltpu.VMEM((TIME, ROWS, FIRST, C), BF),
            pltpu.VMEM((TIME, (ROWS + 2) * WIDE, C), BF),
            pltpu.VMEM((TIME, ROWS * IW, C), F32),
            pltpu.VMEM((3, ROWS * FIRST, C), BF),
            pltpu.VMEM((TIME, 3, ROWS * WIDE, C), BF),
            pltpu.VMEM((2, TIME, 3, ROWS * WIDE, C), BF),
            pltpu.VMEM((2, TIME, ROWS * FW, C), F32),
            pltpu.VMEM((2, ROWS * WIDE, C), F32),
            pltpu.VMEM(((CY + 4) * WIDE, 4 * C), F32),
            pltpu.VMEM(((CY + 2) * WIDE, 4 * C), F32),
            pltpu.VMEM((2, 3, 3, 2 * C, 4 * C), BF),
            pltpu.VMEM((2, 8, 4 * C), F32),
            pltpu.VMEM((2, TIME, CY, HALF * C), BF),
            pltpu.VMEM((2, CY, HALF * C), F32),
            dma((12,)),
            dma((3,)),
            dma((3,)),
            dma((TIME, 5)),
            dma((TIME, 5)),
            dma((TIME, 5)),
            dma((TIME, 5)),
            dma((TIME + 1,)),
            dma((TIME + 1,)),
        ],
        compiler_params=pltpu.CompilerParams(
            collective_id=0, has_side_effects=True, vmem_limit_bytes=58 * 2**20
        ),
    )(frames, weights, bias)


def solution(mesh):
    return jax.shard_map(
        local,
        mesh=mesh,
        in_specs=(P(None, "tile", None, None), P("section", None, None, None, None), P("section", None)),
        out_specs=(P("section", None, "tile", None, None), P("section", "tile", None, None)),
        check_vma=False,
    )
```
